128 devices in a mesh: fn: 4 (over z), se: 32 (over x, y, core).
Axes of the slice: x: 4, y: 4, z: 4, core: 2. Of those that a mesh axis runs over, the one named last changes fastest.
Arguments:
- iface_adj: bfloat16 [384, 98304], P(('fn', 'se')), may hold values from -6 to 6
- panels: bfloat16 [512, 1536, 1536], P('se', 'fn'), may hold values from -0.15625 to 0.15625
- block_mask: int32 [512, 16, 16], P('se', 'fn'), may hold values 0 or 1
- connectivity: int32 [512, 16], P('se'), may hold values from 0 to 31, as said below
- var_map: int32 [512, 16], P('se', 'fn'), may hold values from 0 to 2047
- state_terms: float32 [512, 1536], P('se', 'fn'), may hold values from -0.24 to 0.24
Outputs:
- interior_adj: bfloat16 [512, 384, 1536], P('se', None, 'fn')
- thickness_grad: float32 [384, 2048], P(('fn', 'se'))
The draws below stay inside these ranges and needn't reach their ends.
Inputs may be any that keep to these rules, and one draw needn't show every extreme that they name: `connectivity`: each row names 16 different interface blocks of its own group.
All inputs are finite; a program needn't handle non-finite values. No bound on the sum of `block_mask` on one device may be relied on, other than what follows from the above.
Results may differ from the reference program's by a relative error of at most 0.001.
Values may be sent and summed in bfloat16 or wider, within the bound.
A program may use at most 192 MiB of HBM per device.

```python
import jax
import jax.numpy as jnp
from jax import lax

F = 384
NB = 96
NBLK = 16
NV = 2048
SE_DEV = 16
IB_DEV = 32
M = 1536
SE = 512
NI = 98304


def draw_connectivity(key, part):
    keys = jax.random.split(key, SE)

    def choose(sub_key):
        return jax.random.permutation(sub_key, IB_DEV)[:NBLK]
    return jax.vmap(choose)(keys).astype(jnp.int32)


def with_ends(values, rng, least, top_value):
    place = [jax.random.randint(jax.random.fold_in(rng, axis), (), 0, length) for axis, length in enumerate(values.shape)]
    widest = values.shape.index(max(values.shape))
    next_to = place[:widest] + [(place[widest] + 1) % values.shape[widest]] + place[widest + 1:]
    return values.at[tuple(place)].set(least).at[tuple(next_to)].set(top_value)


def steps_of(stream_key, dims, shards, low, high):
    loudness = 1.0
    for position, shards_of in shards:
        steps = jax.random.uniform(jax.random.fold_in(jax.random.fold_in(stream_key, 6), position), (shards_of,), jnp.float32, low / len(shards), high / len(shards))
        loudness = loudness * jnp.repeat(jnp.exp(steps), dims[position] // shards_of).reshape((-1,) + (1,) * (len(dims) - 1 - position))
    return loudness


def gaussian(key, shape, scale, limit, cuts=(), held_as=jnp.bfloat16):
    factor_of = steps_of(key, shape, cuts, -0.22, 0.18) if cuts else 1.0
    result = jax.random.normal(key, shape, jnp.float32) * scale * factor_of
    return jnp.minimum(jnp.maximum(result, -limit), limit).astype(held_as)


def setup_inputs(seed: int = 0) -> dict:
    seeds = jax.random.split(jax.random.key(seed), 7)
    iface_adj = gaussian(seeds[0], (F, NI), 1.0, 6.0, ((0, 128),))
    panels = gaussian(seeds[1], (SE, M, M), M ** -0.5, 0.15625, ((0, 32), (1, 4)))
    block_mask = with_ends((jax.random.randint(seeds[2], (SE, NBLK, NBLK), 0, 4) < 3).astype(jnp.int32), jax.random.fold_in(seeds[2], 1), 0, 1)
    connectivity = draw_connectivity(jax.random.fold_in(seeds[6], 71), 0)
    var_map = with_ends(jax.random.randint(seeds[4], (SE, NBLK), 0, NV), jax.random.fold_in(seeds[4], 1), 0, NV - 1).astype(jnp.int32)
    state_terms = gaussian(seeds[5], (SE, M), 0.04, 0.24, ((0, 32), (1, 4)), jnp.float32)
    return {"iface_adj": iface_adj, "panels": panels, "block_mask": block_mask, "connectivity": connectivity, "var_map": var_map, "state_terms": state_terms}


def reference(iface_adj, panels, block_mask, connectivity, var_map, state_terms):
    iface_pool = iface_adj.reshape(F, -1, NB)
    variables = jnp.arange(NV, dtype=jnp.int32)

    def single(gradient, inputs):
        se_index, matrix, pattern, linked, targets, weights = inputs
        group_id = se_index // SE_DEV
        boundary = jnp.take(iface_pool, group_id * IB_DEV + linked, axis=1).reshape(F, NBLK * NB)
        blocks = matrix.reshape(NBLK, NB, NBLK, NB) * pattern.astype(matrix.dtype)[:, None, :, None]
        blocks = blocks.reshape(NBLK * NB, NBLK * NB)
        interior = -jnp.dot(boundary, blocks.T, preferred_element_type=jnp.float32)
        block_sums = jnp.sum(interior.reshape(F, NBLK, NB) * weights.reshape(1, NBLK, NB), axis=2)
        onehot = (targets[:, None] == variables[None, :]).astype(jnp.float32)
        gradient = gradient + jnp.dot(block_sums, onehot, precision=lax.Precision.HIGHEST)
        return gradient, interior.astype(jnp.bfloat16)

    se_ids = jnp.arange(SE, dtype=jnp.int32)
    gradient, interior_adj = lax.scan(single, jnp.zeros((F, NV), jnp.float32),
                                      (se_ids, panels, block_mask, connectivity, var_map, state_terms))
    return interior_adj, gradient
```

```python
import jax
import jax.numpy as jnp
from jax import lax
from jax.experimental import pallas as pl
from jax.experimental.pallas import tpu as pltpu
from jax.sharding import PartitionSpec as P

NB = 96
NBLK = 16
NV = 2048
FN = 4
SEA = 32
ROWS = 96
COLS = 3072
FUNCS = FN * ROWS
M = NBLK * NB
LANES = 128
BF16 = jnp.bfloat16
F32 = jnp.float32
MESH = pl.DeviceIdType.MESH
NT = (((1,), (1,)), ((), ()))


def greet(se_peers, fn_peers):
    me, z = lax.axis_index("se"), lax.axis_index("fn")
    barrier = pltpu.get_barrier_semaphore()

    @pl.loop(1, SEA)
    def _(o):
        pl.semaphore_signal(barrier, inc=1, device_id={"se": lax.rem(me + o, SEA)}, device_id_type=MESH)

    for o in fn_peers:
        pl.semaphore_signal(barrier, inc=1, device_id={"fn": lax.rem(z + o, FN)}, device_id_type=MESH)
    pl.semaphore_wait(barrier, SEA - 1 + len(fn_peers))


def gather_kernel(x, out, recv, wide, own, send1, recv1, zsend, zrecv, lsem):
    me, z = lax.axis_index("se"), lax.axis_index("fn")
    greet(SEA, (1, 3))

    def piece(target, source):
        return pltpu.make_async_remote_copy(
            src_ref=x.at[:, pl.ds(pl.multiple_of(target * COLS, COLS), COLS)],
            dst_ref=recv.at[source],
            send_sem=send1.at[target],
            recv_sem=recv1.at[source],
            device_id={"se": target},
            device_id_type=MESH,
        )

    @pl.loop(1, SEA)
    def _(o):
        piece(lax.rem(me + o, SEA), me).start()

    mine = pltpu.make_async_copy(x.at[:, pl.ds(pl.multiple_of(me * COLS, COLS), COLS)], recv.at[me], lsem)
    mine.start()
    mine.wait()

    @pl.loop(1, SEA)
    def _(o):
        source = lax.rem(me + SEA - o, SEA)
        piece(source, source).wait_recv()

    @pl.loop(0, SEA // 8)
    def _(g):
        for u in range(8):
            wide[g, 3 * u : 3 * u + 3, :] = recv[g * 8 + u].astype(F32)

    own[...] = wide[...].reshape(ROWS, COLS).astype(BF16)

    right, left, far = lax.rem(z + 1, FN), lax.rem(z + 3, FN), lax.rem(z + 2, FN)
    half = ROWS // 2

    def slot(owner, h):
        return out.at[pl.ds(pl.multiple_of(owner * ROWS + h * half, half), half), :]

    def send(src, owner, h, target, n):
        return pltpu.make_async_remote_copy(
            src_ref=src,
            dst_ref=slot(owner, h),
            send_sem=zsend.at[n],
            recv_sem=zrecv.at[n],
            device_id={"fn": target},
            device_id_type=MESH,
        )

    def own_half(h):
        return own.at[pl.ds(h * half, half), :]

    r0, r1 = send(own_half(0), z, 0, right, 0), send(own_half(1), z, 1, right, 1)
    l1, l0 = send(own_half(1), z, 1, left, 2), send(own_half(0), z, 0, left, 3)
    r0.start()
    l1.start()
    r1.start()
    l0.start()
    keep = pltpu.make_async_copy(own, out.at[pl.ds(pl.multiple_of(z * ROWS, ROWS), ROWS), :], lsem)
    keep.start()
    r0.wait_recv()
    rr = send(slot(left, 0), left, 0, right, 4)
    rr.start()
    l1.wait_recv()
    ll = send(slot(right, 1), right, 1, left, 5)
    ll.start()
    keep.wait()
    for c in (r1, l0, rr, ll):
        c.wait_recv()
    for c in (r0, r1, l0, l1, rr, ll):
        c.wait_send()

    @pl.loop(1, SEA)
    def _(o):
        piece(lax.rem(me + o, SEA), me).wait_send()


def gather(x):
    return pl.pallas_call(
        gather_kernel,
        out_shape=jax.ShapeDtypeStruct((FUNCS, COLS), BF16),
        in_specs=[pl.BlockSpec(memory_space=pl.ANY)],
        out_specs=pl.BlockSpec(memory_space=pl.ANY),
        scratch_shapes=[
            pltpu.VMEM((SEA, 3, COLS), BF16),
            pltpu.VMEM((SEA // 8, 24, COLS), F32),
            pltpu.VMEM((ROWS, COLS), BF16),
            pltpu.SemaphoreType.DMA((SEA,)),
            pltpu.SemaphoreType.DMA((SEA,)),
            pltpu.SemaphoreType.DMA((6,)),
            pltpu.SemaphoreType.DMA((6,)),
            pltpu.SemaphoreType.DMA,
        ],
        compiler_params=pltpu.CompilerParams(collective_id=0, has_side_effects=True, vmem_limit_bytes=24 << 20),
    )(x)


def panel_kernel(conn, piece, panel, mask, terms, out, sums, rot, expand, bound, masked):
    s = pl.program_id(0)

    @pl.when(s == 0)
    def _():
        sums[...] = jnp.zeros_like(sums)
        block = lax.broadcasted_iota(jnp.int32, (NBLK, M), 1) // NB
        row = lax.broadcasted_iota(jnp.int32, (NBLK, M), 0)
        expand[...] = jnp.where(block == row, -1.0, 0.0).astype(BF16)

        @pl.loop(0, COLS // (4 * NB))
        def _(g):
            cols = piece[:, pl.ds(pl.multiple_of(g * 4 * NB, 4 * NB), 4 * NB)].astype(F32)
            for u in range(4):
                part = cols[:, u * NB : (u + 1) * NB]
                first = jnp.concatenate([part, jnp.zeros((FUNCS, LANES - NB), F32)], axis=1)
                rot[0, g * 4 + u] = first.astype(BF16)
                for r in range(1, 4):
                    rot[r, g * 4 + u] = pltpu.roll(first, LANES - 32 * r, 1).astype(BF16)

    keep = jnp.dot(mask[s].astype(F32).astype(BF16), expand[...], preferred_element_type=F32).astype(BF16)
    for i in range(4):
        masked[i * NB : (i + 1) * NB, :] = panel[0, i * NB : (i + 1) * NB, :] * keep[i : i + 1, :]

    lane = lax.broadcasted_iota(jnp.int32, (FUNCS, LANES), 1)
    for g in range(4):
        a, b, c, d = (rot.at[u, conn[s, 4 * g + u]] for u in range(4))
        at = g * 4 * NB
        b_, c_ = b[...], c[...]
        bound[:, at : at + LANES] = jnp.where(lane < 96, a[...], b_)
        bound[:, at + LANES : at + 2 * LANES] = jnp.where(lane < 64, b_, c_)
        bound[:, at + 2 * LANES : at + 3 * LANES] = jnp.where(lane < 32, c_, d[...])

    interior = lax.dot_general(bound[...], masked[...], NT, preferred_element_type=F32)
    high = interior.astype(BF16)
    out[0] = high
    low = (interior - high.astype(F32)).astype(BF16)

    w = terms[pl.ds(s, 1), :]
    w_high = w.astype(BF16).astype(F32)
    row = lax.broadcasted_iota(jnp.int32, (LANES, 4 * NB), 0)
    block = lax.broadcasted_iota(jnp.int32, (LANES, 4 * NB), 1) // NB
    held = jnp.where(row < 64, w_high, w - w_high)
    held = jnp.where((row & 63) == 4 * s + block, held, 0.0).astype(BF16)
    sums[...] += lax.dot_general(
        jnp.concatenate([high, low], axis=1), jnp.concatenate([held, held], axis=1), NT, preferred_element_type=F32
    )

    @pl.when(s == pl.num_programs(0) - 1)
    def _():
        total = sums[...]
        sums[...] = total + pltpu.roll(total, 64, 1)


def panels_step(piece, panels, block_mask, connectivity, state_terms):
    count = panels.shape[0]
    rows = panels.shape[1]
    return pl.pallas_call(
        panel_kernel,
        out_shape=(
            jax.ShapeDtypeStruct((count, FUNCS, rows), BF16),
            jax.ShapeDtypeStruct((FUNCS, LANES), F32),
        ),
        grid_spec=pltpu.PrefetchScalarGridSpec(
            num_scalar_prefetch=1,
            grid=(count,),
            in_specs=[
                pl.BlockSpec((FUNCS, COLS), lambda s, c: (0, 0)),
                pl.BlockSpec((1, rows, M), lambda s, c: (s, 0, 0)),
                pl.BlockSpec((count, 4, NBLK), lambda s, c: (0, 0, 0)),
                pl.BlockSpec((count, rows), lambda s, c: (0, 0)),
            ],
            out_specs=(
                pl.BlockSpec((1, FUNCS, rows), lambda s, c: (s, 0, 0)),
                pl.BlockSpec((FUNCS, LANES), lambda s, c: (0, 0)),
            ),
            scratch_shapes=[
                pltpu.VMEM((4, COLS // NB, FUNCS, LANES), BF16),
                pltpu.VMEM((NBLK, M), BF16),
                pltpu.VMEM((FUNCS, M), BF16),
                pltpu.VMEM((rows, M), BF16),
            ],
        ),
        compiler_params=pltpu.CompilerParams(vmem_limit_bytes=48 << 20),
        cost_estimate=pl.CostEstimate(flops=7_250_000_000, bytes_accessed=27_000_000, transcendentals=0),
    )(connectivity, piece, panels, block_mask, state_terms)


def gradient_kernel(sums, var, out, msg, mid, got, zsend, zrecv, send2, recv2):
    me, z = lax.axis_index("se"), lax.axis_index("fn")
    low_lane = lax.broadcasted_iota(jnp.int32, (LANES, LANES), 1) < 64
    parts = [sums[pl.ds(a, LANES, stride=3), :] for a in range(3)]
    msg[:, 0, :] = jnp.where(low_lane, parts[0], parts[1])
    msg[:, 1, :] = jnp.where(low_lane, parts[2], var[...])
    greet(SEA, (1, 2, 3))

    def along(target, source, n):
        return pltpu.make_async_remote_copy(
            src_ref=msg.at[pl.ds(target * SEA, SEA)],
            dst_ref=mid.at[source],
            send_sem=zsend.at[n],
            recv_sem=zrecv.at[n],
            device_id={"fn": target},
            device_id_type=MESH,
        )

    for o in range(1, FN):
        along(lax.rem(z + o, FN), z, o).start()
    mid[z] = msg[pl.ds(z * SEA, SEA)]
    for o in range(1, FN):
        source = lax.rem(z + FN - o, FN)
        along(source, source, o).wait_recv()

    def across(target, source):
        return pltpu.make_async_remote_copy(
            src_ref=mid.at[:, target],
            dst_ref=got.at[pl.ds(source * FN, FN)],
            send_sem=send2.at[target],
            recv_sem=recv2.at[source],
            device_id={"se": target},
            device_id_type=MESH,
        )

    @pl.loop(1, SEA)
    def _(o):
        across(lax.rem(me + o, SEA), me).start()

    got[pl.ds(me * FN, FN)] = mid[:, me]

    @pl.loop(1, SEA)
    def _(o):
        source = lax.rem(me + SEA - o, SEA)
        across(source, source).wait_recv()

    first, second = got[:, 0, :].T, got[:, 1, :].T
    x = [first[:64], first[64:], second[:64]]
    v = second[64:]
    v_high = jnp.floor(v * (1.0 / 128.0))
    v_low = v - 128.0 * v_high
    group = lax.broadcasted_iota(jnp.int32, (16, 2 * LANES), 0).astype(F32)
    place = lax.broadcasted_iota(jnp.int32, (LANES, 2 * LANES), 0).astype(F32)

    def pair(t, q):
        return jnp.concatenate([t[2 * q : 2 * q + 1], t[2 * q + 1 : 2 * q + 2]], axis=1)

    total = jnp.zeros((96, LANES), F32)
    for q in range(32):
        in_group = group == pair(v_high, q)
        rows = []
        for a in range(3):
            value = pair(x[a], q)
            high = value.astype(BF16).astype(F32)
            rows.append(jnp.where(in_group, high, 0.0).astype(BF16))
            rows.append(jnp.where(in_group, value - high, 0.0).astype(BF16))
        here = jnp.where(place == pair(v_low, q), 1.0, 0.0).astype(BF16)
        total += lax.dot_general(jnp.concatenate(rows, axis=0), here, NT, preferred_element_type=F32)
    for a in range(3):
        out[a] = total[32 * a : 32 * a + 16] + total[32 * a + 16 : 32 * a + 32]

    for o in range(1, FN):
        along(lax.rem(z + o, FN), z, o).wait_send()

    @pl.loop(1, SEA)
    def _(o):
        across(lax.rem(me + o, SEA), me).wait_send()


def gradient(sums, var):
    return pl.pallas_call(
        gradient_kernel,
        out_shape=jax.ShapeDtypeStruct((3, NV // LANES, LANES), F32),
        in_specs=[pl.BlockSpec(memory_space=pltpu.VMEM)] * 2,
        out_specs=pl.BlockSpec(memory_space=pltpu.VMEM),
        scratch_shapes=[
            pltpu.VMEM((FN * SEA, 2, LANES), F32),
            pltpu.VMEM((FN, SEA, 2, LANES), F32),
            pltpu.VMEM((FN * SEA, 2, LANES), F32),
            pltpu.SemaphoreType.DMA((FN,)),
            pltpu.SemaphoreType.DMA((FN,)),
            pltpu.SemaphoreType.DMA((SEA,)),
            pltpu.SemaphoreType.DMA((SEA,)),
        ],
        compiler_params=pltpu.CompilerParams(collective_id=1, has_side_effects=True, vmem_limit_bytes=24 << 20),
    )(sums, var)


def body(iface_adj, panels, block_mask, connectivity, var_map, state_terms):
    piece = gather(iface_adj)
    interior, sums = panels_step(piece, panels, block_mask, connectivity, state_terms)
    var = var_map.astype(F32).reshape(1, 64)
    var = jnp.concatenate([var, var], axis=1)
    grad = gradient(sums, var)
    return interior, grad.reshape(3, NV)


def solution(mesh):
    placed = (
        P(("fn", "se"), None),
        P("se", "fn", None),
        P("se", "fn", None),
        P("se", None),
        P("se", "fn"),
        P("se", "fn"),
    )
    return jax.shard_map(
        body,
        mesh=mesh,
        in_specs=placed,
        out_specs=(P("se", None, "fn"), P(("fn", "se"), None)),
        check_vma=False,
    )
```

```python
import jax
import jax.numpy as jnp
from jax import lax
from jax.experimental import pallas as pl
from jax.experimental.pallas import tpu as pltpu
from jax.sharding import PartitionSpec as P

NB = 96
NBLK = 16
NV = 2048
FN = 4
SEA = 32
ROWS = 96
COLS = 3072
FUNCS = FN * ROWS
M = NBLK * NB
LANES = 128
BF16 = jnp.bfloat16
F32 = jnp.float32
MESH = pl.DeviceIdType.MESH
NT = (((1,), (1,)), ((), ()))
WIDE = 512
LIMIT_A = 12
LIMIT_B = 12
CHUNKS = 4
PART = COLS // CHUNKS
HALF = ROWS // 2


def gather_kernel(
    x, panels, mask_in, terms_in, pext, rot, recv, wide, planes, mask, terms, expand,
    small, psem, send1, recv1, zsend, zrecv,
):
    me, z = lax.axis_index("se"), lax.axis_index("fn")
    right, left, far = lax.rem(z + 1, FN), lax.rem(z + 3, FN), lax.rem(z + 2, FN)
    count = panels.shape[0]

    barrier = pltpu.get_barrier_semaphore()

    @pl.loop(1, SEA)
    def _(o):
        pl.semaphore_signal(barrier, inc=1, device_id={"se": lax.rem(me + o, SEA)}, device_id_type=MESH)

    for t in (right, left):
        pl.semaphore_signal(barrier, inc=1, device_id={"fn": t}, device_id_type=MESH)

    def columns(target, q):
        return x.at[:, pl.ds(pl.multiple_of(target * COLS + q * PART, PART), PART)]

    smalls = [
        pltpu.make_async_copy(a, b, small.at[n]) for n, (a, b) in enumerate(((mask_in, mask), (terms_in, terms)))
    ]
    mine = [pltpu.make_async_copy(columns(me, q), recv.at[q, me], small.at[2 + q]) for q in range(CHUNKS)]
    for c in (*smalls, *mine):
        c.start()

    def panel(s):
        return pltpu.make_async_copy(panels.at[s], pext.at[s, pl.ds(0, 4 * NB), :], psem.at[s])

    @pl.loop(0, count)
    def _(s):
        panel(s).start()

    pl.semaphore_wait(barrier, SEA - 1 + 2)

    def piece(target, source, q):
        return pltpu.make_async_remote_copy(
            src_ref=columns(target, q),
            dst_ref=recv.at[q, source],
            send_sem=send1.at[q, target],
            recv_sem=recv1.at[q, source],
            device_id={"se": target},
            device_id_type=MESH,
        )

    for q in range(CHUNKS):

        @pl.loop(1, SEA)
        def _(o):
            piece(lax.rem(me + o, SEA), me, q).start()

    for c in smalls:
        c.wait()
    block = lax.broadcasted_iota(jnp.int32, (NBLK, M), 1) // NB
    row = lax.broadcasted_iota(jnp.int32, (NBLK, M), 0)
    expand[...] = jnp.where(block == row, -1.0, 0.0).astype(BF16)

    def prepare(s):
        panel(s).wait()
        keep = jnp.dot(mask[s].astype(F32).astype(BF16), expand[...], preferred_element_type=F32).astype(BF16)
        for i in range(4):
            rows = pl.ds(i * NB, NB)
            pext[s, rows, :] = pext[s, rows, :] * keep[i : i + 1, :]
        w = terms[pl.ds(s, 1), :]
        w_high = w.astype(BF16).astype(F32)
        at = lax.broadcasted_iota(jnp.int32, (LANES, 4 * NB), 0)
        of = lax.broadcasted_iota(jnp.int32, (LANES, 4 * NB), 1) // NB
        held = jnp.where(at < 64, w_high, w - w_high)
        held = jnp.where((at & 63) == 4 * s + of, held, 0.0).astype(BF16)
        both = jnp.dot(held, pext[s, pl.ds(0, 4 * NB), :], preferred_element_type=F32)
        total = both[:64] + both[64:]
        high = total.astype(BF16)
        pext[s, pl.ds(4 * NB, 64), :] = high
        pext[s, pl.ds(4 * NB + 64, 64), :] = (total - high.astype(F32)).astype(BF16)

    def pack(q):
        mine[q].wait()

        @pl.loop(1, SEA)
        def _(o):
            source = lax.rem(me + SEA - o, SEA)
            piece(source, source, q).wait_recv()

        @pl.loop(0, SEA // 8)
        def _(g):
            for u in range(8):
                wide[g, 3 * u : 3 * u + 3, :] = recv[q, g * 8 + u].astype(F32)

        planes[q, z] = wide[...].reshape(ROWS, PART).astype(BF16)

    def send(owner, h, target, n, q):
        part = planes.at[q, owner, pl.ds(h * HALF, HALF), :]
        return pltpu.make_async_remote_copy(
            src_ref=part,
            dst_ref=part,
            send_sem=zsend.at[6 * q + n],
            recv_sem=zrecv.at[6 * q + n],
            device_id={"fn": target},
            device_id_type=MESH,
        )

    def sends(q):
        return [send(z, 0, right, 0, q), send(z, 1, left, 2, q), send(z, 1, right, 1, q), send(z, 0, left, 3, q)]

    def onward(q):
        return send(left, 0, right, 4, q)

    def backward(q):
        return send(right, 1, left, 5, q)

    def relay(q):
        send(left, 0, right, 0, q).wait_recv()
        onward(q).start()
        send(right, 1, left, 2, q).wait_recv()
        backward(q).start()

    def rotate(owner, q):
        @pl.loop(0, PART // (4 * NB))
        def _(g):
            cols = planes[q, owner, :, pl.ds(pl.multiple_of(g * 4 * NB, 4 * NB), 4 * NB)].astype(F32)
            rows = pl.ds(pl.multiple_of(owner * ROWS, ROWS), ROWS)
            for u in range(4):
                part = cols[:, u * NB : (u + 1) * NB]
                first = jnp.concatenate([part, jnp.zeros((ROWS, LANES - NB), F32)], axis=1)
                for r in range(4):
                    turned = first if r == 0 else pltpu.roll(first, LANES - 32 * r, 1)
                    rot[r, q * (PART // NB) + g * 4 + u, rows, :] = turned.astype(BF16)

    for q in range(CHUNKS):
        pl.loop(q * (count // CHUNKS), (q + 1) * (count // CHUNKS))(prepare)
        pack(q)
        for c in sends(q):
            c.start()
        if q:
            relay(q - 1)
        rotate(z, q)
    relay(CHUNKS - 1)
    for q in range(CHUNKS):
        send(left, 1, right, 1, q).wait_recv()
        rotate(left, q)
        send(right, 0, left, 3, q).wait_recv()
        rotate(right, q)
    for q in range(CHUNKS):
        send(far, 0, right, 4, q).wait_recv()
        send(far, 1, left, 5, q).wait_recv()
        rotate(far, q)
    for q in range(CHUNKS):
        for c in (*sends(q), onward(q), backward(q)):
            c.wait_send()

        @pl.loop(1, SEA)
        def _(o):
            piece(lax.rem(me + o, SEA), me, q).wait_send()


def panel_kernel(rot, pext, conn, out, sums, stage, osem):
    lane = lax.broadcasted_iota(jnp.int32, (FUNCS, LANES), 1)
    count = out.shape[0]

    def store(s, k):
        return pltpu.make_async_copy(stage.at[k], out.at[s], osem.at[k])

    sums[...] = jnp.zeros_like(sums)

    @pl.loop(0, count // 2)
    def _(pair):
        for k in range(2):
            s = 2 * pair + k
            tiles = []
            for g in range(4):
                a, b, c, d = (rot[u, conn[s, 4 * g + u]] for u in range(4))
                tiles += [jnp.where(lane < 96, a, b), jnp.where(lane < 64, b, c), jnp.where(lane < 32, c, d)]
            bound = jnp.concatenate(tiles, axis=1)
            found = lax.dot_general(bound, pext[s], NT, preferred_element_type=F32)

            @pl.when(pair > 0)
            def _():
                store(s, k).wait()

            stage[k] = found[:, : 4 * NB].astype(BF16)
            store(s, k).start()
            sums[...] += found[:, 4 * NB :]

    for k in range(2):
        store(k, k).wait()
    total = sums[...]
    sums[...] = total + pltpu.roll(total, 64, 1)


def gradient_kernel(sums, var, out, msg, mid, turned, got, zsend, zrecv, send2, recv2):
    me, z = lax.axis_index("se"), lax.axis_index("fn")
    barrier = pltpu.get_barrier_semaphore()

    @pl.loop(1, SEA)
    def _(o):
        pl.semaphore_signal(barrier, inc=1, device_id={"se": lax.rem(me + o, SEA)}, device_id_type=MESH)

    for o in range(1, FN):
        pl.semaphore_signal(barrier, inc=1, device_id={"fn": lax.rem(z + o, FN)}, device_id_type=MESH)

    v = var[...].astype(F32)
    v_high = jnp.floor(v * (1.0 / 128.0))
    v_low = v - 128.0 * v_high
    lane16 = lax.broadcasted_iota(jnp.int32, (NBLK, LANES), 1)
    row16 = lax.broadcasted_iota(jnp.int32, (NBLK, LANES), 0)
    spread = jnp.where((lane16 & 63) // 4 == row16, 1.0, 0.0).astype(BF16)
    ids = 128.0 * jnp.dot(v_high.astype(BF16), spread, preferred_element_type=F32) + jnp.dot(
        v_low.astype(BF16), spread, preferred_element_type=F32
    )
    lane4 = lax.broadcasted_iota(jnp.int32, (4, LANES), 1)
    row4 = lax.broadcasted_iota(jnp.int32, (4, LANES), 0)
    ids = jnp.sum(jnp.where((lane4 & 3) == row4, ids, 0.0), axis=0, keepdims=True)

    low_lane = lax.broadcasted_iota(jnp.int32, (SEA, LANES), 1) < 64
    for t in range(FN):
        parts = [sums[pl.ds(t * ROWS + a, SEA, stride=3), :] for a in range(3)]
        msg[t, pl.ds(0, SEA, stride=2), :] = jnp.where(low_lane, parts[0], parts[1])
        msg[t, pl.ds(1, SEA, stride=2), :] = jnp.where(low_lane, parts[2], ids)
    pl.semaphore_wait(barrier, SEA - 1 + 3)

    def along(target, source, n):
        return pltpu.make_async_remote_copy(
            src_ref=msg.at[target],
            dst_ref=mid.at[source],
            send_sem=zsend.at[n],
            recv_sem=zrecv.at[n],
            device_id={"fn": target},
            device_id_type=MESH,
        )

    for o in (2, 1, 3):
        along(lax.rem(z + o, FN), z, o).start()
    mid[z] = msg[z]
    for o in (1, 3, 2):
        along(z, lax.rem(z + FN - o, FN), o).wait_recv()
    for t in range(FN):
        for h in range(2):
            turned[pl.ds(2 * t + h, SEA, stride=8), :] = mid[t, pl.ds(h, SEA, stride=2), :]

    def across(target, source):
        return pltpu.make_async_remote_copy(
            src_ref=turned.at[pl.ds(pl.multiple_of(target * 8, 8), 8)],
            dst_ref=got.at[pl.ds(pl.multiple_of(source * 8, 8), 8)],
            send_sem=send2.at[target],
            recv_sem=recv2.at[source],
            device_id={"se": target},
            device_id_type=MESH,
        )

    @pl.loop(1, SEA)
    def _(o):
        across(lax.rem(me + o, SEA), me).start()

    own = pl.ds(pl.multiple_of(me * 8, 8), 8)
    got[own] = turned[own]

    @pl.loop(1, SEA)
    def _(o):
        source = lax.rem(me + SEA - o, SEA)
        across(source, source).wait_recv()

    first, second = got[pl.ds(0, LANES, stride=2), :].T, got[pl.ds(1, LANES, stride=2), :].T
    x = [first[:64], first[64:], second[:64]]
    v = second[64:]
    v_high = jnp.floor(v * (1.0 / 128.0))
    v_low = v - 128.0 * v_high
    group = lax.broadcasted_iota(jnp.int32, (16, 2 * LANES), 0).astype(F32)
    place = lax.broadcasted_iota(jnp.int32, (LANES, 2 * LANES), 0).astype(F32)

    def pair(t, q):
        return jnp.concatenate([t[2 * q : 2 * q + 1], t[2 * q + 1 : 2 * q + 2]], axis=1)

    total = jnp.zeros((96, LANES), F32)
    for q in range(32):
        in_group = group == pair(v_high, q)
        rows = []
        for a in range(3):
            value = pair(x[a], q)
            high = value.astype(BF16).astype(F32)
            rows.append(jnp.where(in_group, high, 0.0).astype(BF16))
            rows.append(jnp.where(in_group, value - high, 0.0).astype(BF16))
        here = jnp.where(place == pair(v_low, q), 1.0, 0.0).astype(BF16)
        total += lax.dot_general(jnp.concatenate(rows, axis=0), here, NT, preferred_element_type=F32)
    for a in range(3):
        out[a] = total[32 * a : 32 * a + 16] + total[32 * a + 16 : 32 * a + 32]

    for o in range(1, FN):
        along(lax.rem(z + o, FN), z, o).wait_send()

    @pl.loop(1, SEA)
    def _(o):
        across(lax.rem(me + o, SEA), me).wait_send()


def body(iface_adj, panels, block_mask, connectivity, var_map, state_terms):
    count, rows = panels.shape[0], panels.shape[1]
    hbm = pl.BlockSpec(memory_space=pltpu.HBM)
    vmem = pl.BlockSpec(memory_space=pltpu.VMEM)
    dma = pltpu.SemaphoreType.DMA
    far_operands = [pltpu.with_memory_space_constraint(a, pltpu.HBM) for a in (iface_adj, panels, block_mask, state_terms)]
    pext, rot = pl.pallas_call(
        gather_kernel,
        out_shape=(
            pltpu.VMEM((count, WIDE, M), BF16),
            pltpu.VMEM((4, COLS // NB, FUNCS, LANES), BF16),
        ),
        in_specs=[hbm] * 4,
        out_specs=(vmem, vmem),
        scratch_shapes=[
            pltpu.VMEM((CHUNKS, SEA, 3, PART), BF16),
            pltpu.VMEM((SEA // 8, 24, PART), F32),
            pltpu.VMEM((CHUNKS, FN, ROWS, PART), BF16),
            pltpu.VMEM(block_mask.shape, jnp.int32),
            pltpu.VMEM(state_terms.shape, F32),
            pltpu.VMEM((NBLK, M), BF16),
            dma((2 + CHUNKS,)),
            dma((count,)),
            dma((CHUNKS, SEA)),
            dma((CHUNKS, SEA)),
            dma((6 * CHUNKS,)),
            dma((6 * CHUNKS,)),
        ],
        compiler_params=pltpu.CompilerParams(collective_id=0, has_side_effects=True, vmem_limit_bytes=LIMIT_A << 20),
    )(*far_operands)
    interior, sums = pl.pallas_call(
        panel_kernel,
        out_shape=(
            jax.ShapeDtypeStruct((count, FUNCS, rows), BF16),
            pltpu.VMEM((FUNCS, LANES), F32),
        ),
        in_specs=[vmem, vmem, pl.BlockSpec(memory_space=pltpu.SMEM)],
        out_specs=(pl.BlockSpec(memory_space=pl.ANY), vmem),
        scratch_shapes=[pltpu.VMEM((2, FUNCS, rows), BF16), dma((2,))],
        compiler_params=pltpu.CompilerParams(vmem_limit_bytes=LIMIT_B << 20),
        cost_estimate=pl.CostEstimate(flops=9_700_000_000, bytes_accessed=5_000_000, transcendentals=0),
    )(rot, pext, connectivity)
    grad = pl.pallas_call(
        gradient_kernel,
        out_shape=jax.ShapeDtypeStruct((3, NV // LANES, LANES), F32),
        in_specs=[vmem, vmem],
        out_specs=vmem,
        scratch_shapes=[
            pltpu.VMEM((FN, 2 * SEA, LANES), F32),
            pltpu.VMEM((FN, 2 * SEA, LANES), F32),
            pltpu.VMEM((8 * SEA, LANES), F32),
            pltpu.VMEM((8 * SEA, LANES), F32),
            dma((FN,)),
            dma((FN,)),
            dma((SEA,)),
            dma((SEA,)),
        ],
        compiler_params=pltpu.CompilerParams(collective_id=1, has_side_effects=True, vmem_limit_bytes=8 << 20),
    )(sums, var_map.T)
    return interior, grad.reshape(3, NV)


def solution(mesh):
    placed = (
        P(("fn", "se"), None),
        P("se", "fn", None),
        P("se", "fn", None),
        P("se", None),
        P("se", "fn"),
        P("se", "fn"),
    )
    return jax.shard_map(
        body,
        mesh=mesh,
        in_specs=placed,
        out_specs=(P("se", None, "fn"), P(("fn", "se"), None)),
        check_vma=False,
    )
```

```python
import jax
import jax.numpy as jnp
from jax import lax
from jax.experimental import pallas as pl
from jax.experimental.pallas import tpu as pltpu
from jax.sharding import PartitionSpec as P

NB = 96
NBLK = 16
NV = 2048
FN = 4
SEA = 32
ROWS = 96
COLS = 3072
FUNCS = FN * ROWS
M = NBLK * NB
LANES = 128
BF16 = jnp.bfloat16
F32 = jnp.float32
MESH = pl.DeviceIdType.MESH
NT = (((1,), (1,)), ((), ()))
WIDE = 512
LIMIT_A = 12
LIMIT_B = 12
CHUNKS = 2
EARLY = 4
APART = 6
UNROLL = 4
PART = COLS // CHUNKS
HALF = ROWS // 2


def gather_kernel(
    x, panels, mask_in, terms_in, pext, rot, recv, wide, planes, mask, terms, expand,
    small, psem, send1, recv1, zsend, zrecv,
):
    me, z = lax.axis_index("se"), lax.axis_index("fn")
    right, left, far = lax.rem(z + 1, FN), lax.rem(z + 3, FN), lax.rem(z + 2, FN)
    count = panels.shape[0]

    barrier = pltpu.get_barrier_semaphore()

    @pl.loop(1, SEA)
    def _(o):
        pl.semaphore_signal(barrier, inc=1, device_id={"se": lax.rem(me + o, SEA)}, device_id_type=MESH)

    for t in (right, left):
        pl.semaphore_signal(barrier, inc=1, device_id={"fn": t}, device_id_type=MESH)

    def columns(target, q):
        return x.at[:, pl.ds(pl.multiple_of(target * COLS + q * PART, PART), PART)]

    smalls = [
        pltpu.make_async_copy(a, b, small.at[n]) for n, (a, b) in enumerate(((mask_in, mask), (terms_in, terms)))
    ]
    mine = [pltpu.make_async_copy(columns(me, q), recv.at[q, me], small.at[2 + q]) for q in range(CHUNKS)]
    for c in (*smalls, *mine):
        c.start()

    def panel(s):
        return pltpu.make_async_copy(panels.at[s], pext.at[s, pl.ds(0, 4 * NB), :], psem.at[s])

    @pl.loop(0, count)
    def _(s):
        panel(s).start()

    def piece(target, source, q):
        return pltpu.make_async_remote_copy(
            src_ref=columns(target, q),
            dst_ref=recv.at[q, source],
            send_sem=send1.at[q, target],
            recv_sem=recv1.at[q, source],
            device_id={"se": target},
            device_id_type=MESH,
        )

    def issue(q):
        @pl.loop(1, SEA)
        def _(o):
            piece(lax.rem(me + o, SEA), me, q).start()

    for c in smalls:
        c.wait()
    block = lax.broadcasted_iota(jnp.int32, (NBLK, M), 1) // NB
    row = lax.broadcasted_iota(jnp.int32, (NBLK, M), 0)
    expand[...] = jnp.where(block == row, -1.0, 0.0).astype(BF16)

    def prepare(s):
        panel(s).wait()
        keep = jnp.dot(mask[s].astype(F32).astype(BF16), expand[...], preferred_element_type=F32).astype(BF16)
        for i in range(4):
            rows = pl.ds(i * NB, NB)
            pext[s, rows, :] = pext[s, rows, :] * keep[i : i + 1, :]
        w = terms[pl.ds(s, 1), :]
        w_high = w.astype(BF16).astype(F32)
        at = lax.broadcasted_iota(jnp.int32, (LANES, 4 * NB), 0)
        of = lax.broadcasted_iota(jnp.int32, (LANES, 4 * NB), 1) // NB
        held = jnp.where(at < 64, w_high, w - w_high)
        held = jnp.where((at & 63) == 4 * s + of, held, 0.0).astype(BF16)
        both = jnp.dot(held, pext[s, pl.ds(0, 4 * NB), :], preferred_element_type=F32)
        total = both[:64] + both[64:]
        high = total.astype(BF16)
        pext[s, pl.ds(4 * NB, 64), :] = high
        pext[s, pl.ds(4 * NB + 64, 64), :] = (total - high.astype(F32)).astype(BF16)

    pl.loop(0, EARLY)(prepare)
    pl.semaphore_wait(barrier, SEA - 1 + 2)
    for q in range(CHUNKS):
        issue(q)
        pl.loop(EARLY + q * APART, EARLY + (q + 1) * APART)(prepare)
    done = EARLY + CHUNKS * APART

    def pack(q):
        mine[q].wait()

        @pl.loop(1, SEA)
        def _(o):
            source = lax.rem(me + SEA - o, SEA)
            piece(source, source, q).wait_recv()

        @pl.loop(0, SEA // 8)
        def _(g):
            for u in range(8):
                wide[g, 3 * u : 3 * u + 3, :] = recv[q, g * 8 + u].astype(F32)

        planes[q, z] = wide[...].reshape(ROWS, PART).astype(BF16)

    def send(owner, h, target, n, q):
        part = planes.at[q, owner, pl.ds(h * HALF, HALF), :]
        return pltpu.make_async_remote_copy(
            src_ref=part,
            dst_ref=part,
            send_sem=zsend.at[6 * q + n],
            recv_sem=zrecv.at[6 * q + n],
            device_id={"fn": target},
            device_id_type=MESH,
        )

    def sends(q):
        return [send(z, 0, right, 0, q), send(z, 1, left, 2, q), send(z, 1, right, 1, q), send(z, 0, left, 3, q)]

    def onward(q):
        return send(left, 0, right, 4, q)

    def backward(q):
        return send(right, 1, left, 5, q)

    def relay(q):
        send(left, 0, right, 0, q).wait_recv()
        onward(q).start()
        send(right, 1, left, 2, q).wait_recv()
        backward(q).start()

    def rotate(owner, q):
        @pl.loop(0, PART // (4 * NB))
        def _(g):
            cols = planes[q, owner, :, pl.ds(pl.multiple_of(g * 4 * NB, 4 * NB), 4 * NB)].astype(F32)
            rows = pl.ds(pl.multiple_of(owner * ROWS, ROWS), ROWS)
            for u in range(4):
                part = cols[:, u * NB : (u + 1) * NB]
                first = jnp.concatenate([part, jnp.zeros((ROWS, LANES - NB), F32)], axis=1)
                for r in range(4):
                    turned = first if r == 0 else pltpu.roll(first, LANES - 32 * r, 1)
                    rot[r, q * (PART // NB) + g * 4 + u, rows, :] = turned.astype(BF16)

    for q in range(CHUNKS):
        pack(q)
        for c in sends(q):
            c.start()
        if q == 0:
            pl.loop(done, count)(prepare)
        if q:
            relay(q - 1)
        rotate(z, q)
    relay(CHUNKS - 1)
    for q in range(CHUNKS):

        @pl.loop(1, SEA)
        def _(o):
            piece(lax.rem(me + o, SEA), me, q).wait_send()
    for q in range(CHUNKS):
        send(left, 1, right, 1, q).wait_recv()
        rotate(left, q)
        send(right, 0, left, 3, q).wait_recv()
        rotate(right, q)
    for q in range(CHUNKS):
        send(far, 0, right, 4, q).wait_recv()
        send(far, 1, left, 5, q).wait_recv()
        rotate(far, q)
    for q in range(CHUNKS):
        for c in (*sends(q), onward(q), backward(q)):
            c.wait_send()


def panel_kernel(rot, pext, conn, out, sums, stage, osem):
    lane = lax.broadcasted_iota(jnp.int32, (FUNCS, LANES), 1)
    count = out.shape[0]

    def store(s, k):
        return pltpu.make_async_copy(stage.at[k], out.at[s], osem.at[k])

    sums[...] = jnp.zeros_like(sums)

    @pl.loop(0, count // UNROLL)
    def _(turn):
        for k in range(UNROLL):
            s = UNROLL * turn + k
            tiles = []
            for g in range(4):
                a, b, c, d = (rot[u, conn[s, 4 * g + u]] for u in range(4))
                tiles += [jnp.where(lane < 96, a, b), jnp.where(lane < 64, b, c), jnp.where(lane < 32, c, d)]
            bound = jnp.concatenate(tiles, axis=1)
            found = lax.dot_general(bound, pext[s], NT, preferred_element_type=F32)

            @pl.when(turn > 0)
            def _():
                store(s, k).wait()

            stage[k] = found[:, : 4 * NB].astype(BF16)
            store(s, k).start()
            sums[...] += found[:, 4 * NB :]

    for k in range(UNROLL):
        store(k, k).wait()
    total = sums[...]
    sums[...] = total + pltpu.roll(total, 64, 1)


def gradient_kernel(sums, var, out, msg, mid, turned, got, zsend, zrecv, send2, recv2):
    me, z = lax.axis_index("se"), lax.axis_index("fn")
    barrier = pltpu.get_barrier_semaphore()

    @pl.loop(1, SEA)
    def _(o):
        pl.semaphore_signal(barrier, inc=1, device_id={"se": lax.rem(me + o, SEA)}, device_id_type=MESH)

    for o in range(1, FN):
        pl.semaphore_signal(barrier, inc=1, device_id={"fn": lax.rem(z + o, FN)}, device_id_type=MESH)

    v = var[...].astype(F32)
    v_high = jnp.floor(v * (1.0 / 128.0))
    v_low = v - 128.0 * v_high
    lane16 = lax.broadcasted_iota(jnp.int32, (NBLK, LANES), 1)
    row16 = lax.broadcasted_iota(jnp.int32, (NBLK, LANES), 0)
    spread = jnp.where((lane16 & 63) // 4 == row16, 1.0, 0.0).astype(BF16)
    ids = 128.0 * jnp.dot(v_high.astype(BF16), spread, preferred_element_type=F32) + jnp.dot(
        v_low.astype(BF16), spread, preferred_element_type=F32
    )
    lane4 = lax.broadcasted_iota(jnp.int32, (4, LANES), 1)
    row4 = lax.broadcasted_iota(jnp.int32, (4, LANES), 0)
    ids = jnp.sum(jnp.where((lane4 & 3) == row4, ids, 0.0), axis=0, keepdims=True)

    low_lane = lax.broadcasted_iota(jnp.int32, (SEA, LANES), 1) < 64
    for t in range(FN):
        parts = [sums[pl.ds(t * ROWS + a, SEA, stride=3), :] for a in range(3)]
        msg[t, pl.ds(0, SEA, stride=2), :] = jnp.where(low_lane, parts[0], parts[1])
        msg[t, pl.ds(1, SEA, stride=2), :] = jnp.where(low_lane, parts[2], ids)
    pl.semaphore_wait(barrier, SEA - 1 + 3)

    def along(target, source, n):
        return pltpu.make_async_remote_copy(
            src_ref=msg.at[target],
            dst_ref=mid.at[source],
            send_sem=zsend.at[n],
            recv_sem=zrecv.at[n],
            device_id={"fn": target},
            device_id_type=MESH,
        )

    for o in (2, 1, 3):
        along(lax.rem(z + o, FN), z, o).start()
    mid[z] = msg[z]
    for o in (1, 3, 2):
        along(z, lax.rem(z + FN - o, FN), o).wait_recv()
    for t in range(FN):
        for h in range(2):
            turned[pl.ds(2 * t + h, SEA, stride=8), :] = mid[t, pl.ds(h, SEA, stride=2), :]

    def across(target, source):
        return pltpu.make_async_remote_copy(
            src_ref=turned.at[pl.ds(pl.multiple_of(target * 8, 8), 8)],
            dst_ref=got.at[pl.ds(pl.multiple_of(source * 8, 8), 8)],
            send_sem=send2.at[target],
            recv_sem=recv2.at[source],
            device_id={"se": target},
            device_id_type=MESH,
        )

    @pl.loop(1, SEA)
    def _(o):
        across(lax.rem(me + o, SEA), me).start()

    own = pl.ds(pl.multiple_of(me * 8, 8), 8)
    got[own] = turned[own]

    @pl.loop(1, SEA)
    def _(o):
        source = lax.rem(me + SEA - o, SEA)
        across(source, source).wait_recv()

    first, second = got[pl.ds(0, LANES, stride=2), :].T, got[pl.ds(1, LANES, stride=2), :].T
    x = [first[:64], first[64:], second[:64]]
    v = second[64:]
    v_high = jnp.floor(v * (1.0 / 128.0))
    v_low = v - 128.0 * v_high
    group = lax.broadcasted_iota(jnp.int32, (16, 2 * LANES), 0).astype(F32)
    place = lax.broadcasted_iota(jnp.int32, (LANES, 2 * LANES), 0).astype(F32)

    def pair(t, q):
        return jnp.concatenate([t[2 * q : 2 * q + 1], t[2 * q + 1 : 2 * q + 2]], axis=1)

    total = jnp.zeros((96, LANES), F32)
    for q in range(32):
        in_group = group == pair(v_high, q)
        rows = []
        for a in range(3):
            value = pair(x[a], q)
            high = value.astype(BF16).astype(F32)
            rows.append(jnp.where(in_group, high, 0.0).astype(BF16))
            rows.append(jnp.where(in_group, value - high, 0.0).astype(BF16))
        here = jnp.where(place == pair(v_low, q), 1.0, 0.0).astype(BF16)
        total += lax.dot_general(jnp.concatenate(rows, axis=0), here, NT, preferred_element_type=F32)
    for a in range(3):
        out[a] = total[32 * a : 32 * a + 16] + total[32 * a + 16 : 32 * a + 32]

    for o in range(1, FN):
        along(lax.rem(z + o, FN), z, o).wait_send()

    @pl.loop(1, SEA)
    def _(o):
        across(lax.rem(me + o, SEA), me).wait_send()


def body(iface_adj, panels, block_mask, connectivity, var_map, state_terms):
    count, rows = panels.shape[0], panels.shape[1]
    hbm = pl.BlockSpec(memory_space=pltpu.HBM)
    vmem = pl.BlockSpec(memory_space=pltpu.VMEM)
    dma = pltpu.SemaphoreType.DMA
    far_operands = [pltpu.with_memory_space_constraint(a, pltpu.HBM) for a in (iface_adj, panels, block_mask, state_terms)]
    pext, rot = pl.pallas_call(
        gather_kernel,
        out_shape=(
            pltpu.VMEM((count, WIDE, M), BF16),
            pltpu.VMEM((4, COLS // NB, FUNCS, LANES), BF16),
        ),
        in_specs=[hbm] * 4,
        out_specs=(vmem, vmem),
        scratch_shapes=[
            pltpu.VMEM((CHUNKS, SEA, 3, PART), BF16),
            pltpu.VMEM((SEA // 8, 24, PART), F32),
            pltpu.VMEM((CHUNKS, FN, ROWS, PART), BF16),
            pltpu.VMEM(block_mask.shape, jnp.int32),
            pltpu.VMEM(state_terms.shape, F32),
            pltpu.VMEM((NBLK, M), BF16),
            dma((2 + CHUNKS,)),
            dma((count,)),
            dma((CHUNKS, SEA)),
            dma((CHUNKS, SEA)),
            dma((6 * CHUNKS,)),
            dma((6 * CHUNKS,)),
        ],
        compiler_params=pltpu.CompilerParams(collective_id=0, has_side_effects=True, vmem_limit_bytes=LIMIT_A << 20),
    )(*far_operands)
    interior, sums = pl.pallas_call(
        panel_kernel,
        out_shape=(
            jax.ShapeDtypeStruct((count, FUNCS, rows), BF16),
            pltpu.VMEM((FUNCS, LANES), F32),
        ),
        in_specs=[vmem, vmem, pl.BlockSpec(memory_space=pltpu.SMEM)],
        out_specs=(pl.BlockSpec(memory_space=pl.ANY), vmem),
        scratch_shapes=[pltpu.VMEM((UNROLL, FUNCS, rows), BF16), dma((UNROLL,))],
        compiler_params=pltpu.CompilerParams(vmem_limit_bytes=LIMIT_B << 20),
        cost_estimate=pl.CostEstimate(flops=9_700_000_000, bytes_accessed=5_000_000, transcendentals=0),
    )(rot, pext, connectivity)
    grad = pl.pallas_call(
        gradient_kernel,
        out_shape=jax.ShapeDtypeStruct((3, NV // LANES, LANES), F32),
        in_specs=[vmem, vmem],
        out_specs=vmem,
        scratch_shapes=[
            pltpu.VMEM((FN, 2 * SEA, LANES), F32),
            pltpu.VMEM((FN, 2 * SEA, LANES), F32),
            pltpu.VMEM((8 * SEA, LANES), F32),
            pltpu.VMEM((8 * SEA, LANES), F32),
            dma((FN,)),
            dma((FN,)),
            dma((SEA,)),
            dma((SEA,)),
        ],
        compiler_params=pltpu.CompilerParams(collective_id=1, has_side_effects=True, vmem_limit_bytes=8 << 20),
    )(sums, var_map.T)
    return interior, grad.reshape(3, NV)


def solution(mesh):
    placed = (
        P(("fn", "se"), None),
        P("se", "fn", None),
        P("se", "fn", None),
        P("se", None),
        P("se", "fn"),
        P("se", "fn"),
    )
    return jax.shard_map(
        body,
        mesh=mesh,
        in_specs=placed,
        out_specs=(P("se", None, "fn"), P(("fn", "se"), None)),
        check_vma=False,
    )
```

```python
import jax
import jax.numpy as jnp
from jax import lax
from jax.experimental import pallas as pl
from jax.experimental.pallas import tpu as pltpu
from jax.sharding import PartitionSpec as P

NB = 96
NBLK = 16
NV = 2048
FN = 4
SEA = 32
ROWS = 96
COLS = 3072
FUNCS = FN * ROWS
M = NBLK * NB
LANES = 128
BF16 = jnp.bfloat16
F32 = jnp.float32
MESH = pl.DeviceIdType.MESH
NT = (((1,), (1,)), ((), ()))
WIDE = 512
LIMIT_A = 12
LIMIT_B = 12
CHUNKS = 2
EARLY = 2
APART = 7
UNROLL = 4
PART = COLS // CHUNKS
HALF = ROWS // 2


def gather_kernel(
    x, panels, mask_in, terms_in, pext, rot, recv, wide, planes, mask, terms, expand,
    small, psem, send1, recv1, zsend, zrecv,
):
    me, z = lax.axis_index("se"), lax.axis_index("fn")
    right, left, far = lax.rem(z + 1, FN), lax.rem(z + 3, FN), lax.rem(z + 2, FN)
    count = panels.shape[0]

    barrier = pltpu.get_barrier_semaphore()

    @pl.loop(1, SEA)
    def _(o):
        pl.semaphore_signal(barrier, inc=1, device_id={"se": lax.rem(me + o, SEA)}, device_id_type=MESH)

    for t in (right, left):
        pl.semaphore_signal(barrier, inc=1, device_id={"fn": t}, device_id_type=MESH)

    def columns(target, q):
        return x.at[:, pl.ds(pl.multiple_of(target * COLS + q * PART, PART), PART)]

    smalls = [
        pltpu.make_async_copy(a, b, small.at[n]) for n, (a, b) in enumerate(((mask_in, mask), (terms_in, terms)))
    ]
    mine = [pltpu.make_async_copy(columns(me, q), recv.at[q, me], small.at[2 + q]) for q in range(CHUNKS)]
    for c in (*smalls, *mine):
        c.start()

    def panel(s):
        return pltpu.make_async_copy(panels.at[s], pext.at[s, pl.ds(0, 4 * NB), :], psem.at[s])

    @pl.loop(0, count)
    def _(s):
        panel(s).start()

    def piece(target, source, q):
        return pltpu.make_async_remote_copy(
            src_ref=columns(target, q),
            dst_ref=recv.at[q, source],
            send_sem=send1.at[q, target],
            recv_sem=recv1.at[q, source],
            device_id={"se": target},
            device_id_type=MESH,
        )

    def issue(q):
        @pl.loop(1, SEA)
        def _(o):
            piece(lax.rem(me + o, SEA), me, q).start()

    for c in smalls:
        c.wait()
    block = lax.broadcasted_iota(jnp.int32, (NBLK, M), 1) // NB
    row = lax.broadcasted_iota(jnp.int32, (NBLK, M), 0)
    expand[...] = jnp.where(block == row, -1.0, 0.0).astype(BF16)

    def prepare(s):
        panel(s).wait()
        keep = jnp.dot(mask[s].astype(F32).astype(BF16), expand[...], preferred_element_type=F32).astype(BF16)
        for i in range(4):
            rows = pl.ds(i * NB, NB)
            pext[s, rows, :] = pext[s, rows, :] * keep[i : i + 1, :]
        w = terms[pl.ds(s, 1), :]
        w_high = w.astype(BF16).astype(F32)
        at = lax.broadcasted_iota(jnp.int32, (LANES, 4 * NB), 0)
        of = lax.broadcasted_iota(jnp.int32, (LANES, 4 * NB), 1) // NB
        held = jnp.where(at < 64, w_high, w - w_high)
        held = jnp.where((at & 63) == 4 * s + of, held, 0.0).astype(BF16)
        both = jnp.dot(held, pext[s, pl.ds(0, 4 * NB), :], preferred_element_type=F32)
        total = both[:64] + both[64:]
        high = total.astype(BF16)
        pext[s, pl.ds(4 * NB, 64), :] = high
        pext[s, pl.ds(4 * NB + 64, 64), :] = (total - high.astype(F32)).astype(BF16)

    pl.loop(0, EARLY)(prepare)
    pl.semaphore_wait(barrier, SEA - 1 + 2)
    for q in range(CHUNKS):
        issue(q)
        pl.loop(EARLY + q * APART, EARLY + (q + 1) * APART)(prepare)
    done = EARLY + CHUNKS * APART

    def pack(q):
        mine[q].wait()

        @pl.loop(1, SEA)
        def _(o):
            source = lax.rem(me + SEA - o, SEA)
            piece(source, source, q).wait_recv()

        @pl.loop(0, SEA // 8)
        def _(g):
            for u in range(8):
                wide[g, 3 * u : 3 * u + 3, :] = recv[q, g * 8 + u].astype(F32)

        planes[q, z] = wide[...].reshape(ROWS, PART).astype(BF16)

    def send(owner, h, target, n, q):
        part = planes.at[q, owner, pl.ds(h * HALF, HALF), :]
        return pltpu.make_async_remote_copy(
            src_ref=part,
            dst_ref=part,
            send_sem=zsend.at[6 * q + n],
            recv_sem=zrecv.at[6 * q + n],
            device_id={"fn": target},
            device_id_type=MESH,
        )

    def sends(q):
        return [send(z, 0, right, 0, q), send(z, 1, left, 2, q), send(z, 1, right, 1, q), send(z, 0, left, 3, q)]

    def onward(q):
        return send(left, 0, right, 4, q)

    def backward(q):
        return send(right, 1, left, 5, q)

    def relay(q):
        send(left, 0, right, 0, q).wait_recv()
        onward(q).start()
        send(right, 1, left, 2, q).wait_recv()
        backward(q).start()

    def rotate(owner, q):
        @pl.loop(0, PART // (4 * NB))
        def _(g):
            cols = planes[q, owner, :, pl.ds(pl.multiple_of(g * 4 * NB, 4 * NB), 4 * NB)].astype(F32)
            rows = pl.ds(pl.multiple_of(owner * ROWS, ROWS), ROWS)
            for u in range(4):
                part = cols[:, u * NB : (u + 1) * NB]
                first = jnp.concatenate([part, jnp.zeros((ROWS, LANES - NB), F32)], axis=1)
                for r in range(4):
                    turned = first if r == 0 else pltpu.roll(first, LANES - 32 * r, 1)
                    rot[r, q * (PART // NB) + g * 4 + u, rows, :] = turned.astype(BF16)

    for q in range(CHUNKS):
        if q:
            relay(q - 1)
        pack(q)
        for c in sends(q):
            c.start()
        if q == 0:
            pl.loop(done, count)(prepare)
        rotate(z, q)
    relay(CHUNKS - 1)
    for q in range(CHUNKS):

        @pl.loop(1, SEA)
        def _(o):
            piece(lax.rem(me + o, SEA), me, q).wait_send()
    for q in range(CHUNKS):
        send(left, 1, right, 1, q).wait_recv()
        rotate(left, q)
        send(right, 0, left, 3, q).wait_recv()
        rotate(right, q)
    for q in range(CHUNKS):
        send(far, 0, right, 4, q).wait_recv()
        send(far, 1, left, 5, q).wait_recv()
        rotate(far, q)
    for q in range(CHUNKS):
        for c in (*sends(q), onward(q), backward(q)):
            c.wait_send()


def panel_kernel(rot, pext, conn, out, sums, stage, osem):
    lane = lax.broadcasted_iota(jnp.int32, (FUNCS, LANES), 1)
    count = out.shape[0]

    def store(s, k):
        return pltpu.make_async_copy(stage.at[k], out.at[s], osem.at[k])

    sums[...] = jnp.zeros_like(sums)

    @pl.loop(0, count // UNROLL)
    def _(turn):
        for k in range(UNROLL):
            s = UNROLL * turn + k
            tiles = []
            for g in range(4):
                a, b, c, d = (rot[u, conn[s, 4 * g + u]] for u in range(4))
                tiles += [jnp.where(lane < 96, a, b), jnp.where(lane < 64, b, c), jnp.where(lane < 32, c, d)]
            bound = jnp.concatenate(tiles, axis=1)
            found = lax.dot_general(bound, pext[s], NT, preferred_element_type=F32)

            @pl.when(turn > 0)
            def _():
                store(s, k).wait()

            stage[k] = found[:, : 4 * NB].astype(BF16)
            store(s, k).start()
            sums[...] += found[:, 4 * NB :]

    for k in range(UNROLL):
        store(k, k).wait()
    total = sums[...]
    sums[...] = total + pltpu.roll(total, 64, 1)


def gradient_kernel(sums, var, out, msg, mid, turned, got, zsend, zrecv, send2, recv2):
    me, z = lax.axis_index("se"), lax.axis_index("fn")
    barrier = pltpu.get_barrier_semaphore()

    @pl.loop(1, SEA)
    def _(o):
        pl.semaphore_signal(barrier, inc=1, device_id={"se": lax.rem(me + o, SEA)}, device_id_type=MESH)

    for o in range(1, FN):
        pl.semaphore_signal(barrier, inc=1, device_id={"fn": lax.rem(z + o, FN)}, device_id_type=MESH)

    v = var[...].astype(F32)
    v_high = jnp.floor(v * (1.0 / 128.0))
    v_low = v - 128.0 * v_high
    lane16 = lax.broadcasted_iota(jnp.int32, (NBLK, LANES), 1)
    row16 = lax.broadcasted_iota(jnp.int32, (NBLK, LANES), 0)
    spread = jnp.where((lane16 & 63) // 4 == row16, 1.0, 0.0).astype(BF16)
    ids = 128.0 * jnp.dot(v_high.astype(BF16), spread, preferred_element_type=F32) + jnp.dot(
        v_low.astype(BF16), spread, preferred_element_type=F32
    )
    lane4 = lax.broadcasted_iota(jnp.int32, (4, LANES), 1)
    row4 = lax.broadcasted_iota(jnp.int32, (4, LANES), 0)
    ids = jnp.sum(jnp.where((lane4 & 3) == row4, ids, 0.0), axis=0, keepdims=True)

    low_lane = lax.broadcasted_iota(jnp.int32, (SEA, LANES), 1) < 64
    for t in range(FN):
        parts = [sums[pl.ds(t * ROWS + a, SEA, stride=3), :] for a in range(3)]
        msg[t, pl.ds(0, SEA, stride=2), :] = jnp.where(low_lane, parts[0], parts[1])
        msg[t, pl.ds(1, SEA, stride=2), :] = jnp.where(low_lane, parts[2], ids)
    pl.semaphore_wait(barrier, SEA - 1 + 3)

    def along(target, source, n):
        return pltpu.make_async_remote_copy(
            src_ref=msg.at[target],
            dst_ref=mid.at[source],
            send_sem=zsend.at[n],
            recv_sem=zrecv.at[n],
            device_id={"fn": target},
            device_id_type=MESH,
        )

    for o in (2, 1, 3):
        along(lax.rem(z + o, FN), z, o).start()
    mid[z] = msg[z]
    for o in (1, 3, 2):
        along(z, lax.rem(z + FN - o, FN), o).wait_recv()
    for t in range(FN):
        for h in range(2):
            turned[pl.ds(2 * t + h, SEA, stride=8), :] = mid[t, pl.ds(h, SEA, stride=2), :]

    def across(target, source):
        return pltpu.make_async_remote_copy(
            src_ref=turned.at[pl.ds(pl.multiple_of(target * 8, 8), 8)],
            dst_ref=got.at[pl.ds(pl.multiple_of(source * 8, 8), 8)],
            send_sem=send2.at[target],
            recv_sem=recv2.at[source],
            device_id={"se": target},
            device_id_type=MESH,
        )

    @pl.loop(1, SEA)
    def _(o):
        across(lax.rem(me + o, SEA), me).start()

    own = pl.ds(pl.multiple_of(me * 8, 8), 8)
    got[own] = turned[own]

    @pl.loop(1, SEA)
    def _(o):
        source = lax.rem(me + SEA - o, SEA)
        across(source, source).wait_recv()

    first, second = got[pl.ds(0, LANES, stride=2), :].T, got[pl.ds(1, LANES, stride=2), :].T
    x = [first[:64], first[64:], second[:64]]
    v = second[64:]
    v_high = jnp.floor(v * (1.0 / 128.0))
    v_low = v - 128.0 * v_high
    group = lax.broadcasted_iota(jnp.int32, (16, 2 * LANES), 0).astype(F32)
    place = lax.broadcasted_iota(jnp.int32, (LANES, 2 * LANES), 0).astype(F32)

    def pair(t, q):
        return jnp.concatenate([t[2 * q : 2 * q + 1], t[2 * q + 1 : 2 * q + 2]], axis=1)

    total = jnp.zeros((96, LANES), F32)
    for q in range(32):
        in_group = group == pair(v_high, q)
        rows = []
        for a in range(3):
            value = pair(x[a], q)
            high = value.astype(BF16).astype(F32)
            rows.append(jnp.where(in_group, high, 0.0).astype(BF16))
            rows.append(jnp.where(in_group, value - high, 0.0).astype(BF16))
        here = jnp.where(place == pair(v_low, q), 1.0, 0.0).astype(BF16)
        total += lax.dot_general(jnp.concatenate(rows, axis=0), here, NT, preferred_element_type=F32)
    for a in range(3):
        out[a] = total[32 * a : 32 * a + 16] + total[32 * a + 16 : 32 * a + 32]

    for o in range(1, FN):
        along(lax.rem(z + o, FN), z, o).wait_send()

    @pl.loop(1, SEA)
    def _(o):
        across(lax.rem(me + o, SEA), me).wait_send()


def body(iface_adj, panels, block_mask, connectivity, var_map, state_terms):
    count, rows = panels.shape[0], panels.shape[1]
    hbm = pl.BlockSpec(memory_space=pltpu.HBM)
    vmem = pl.BlockSpec(memory_space=pltpu.VMEM)
    dma = pltpu.SemaphoreType.DMA
    far_operands = [pltpu.with_memory_space_constraint(a, pltpu.HBM) for a in (iface_adj, panels, block_mask, state_terms)]
    pext, rot = pl.pallas_call(
        gather_kernel,
        out_shape=(
            pltpu.VMEM((count, WIDE, M), BF16),
            pltpu.VMEM((4, COLS // NB, FUNCS, LANES), BF16),
        ),
        in_specs=[hbm] * 4,
        out_specs=(vmem, vmem),
        scratch_shapes=[
            pltpu.VMEM((CHUNKS, SEA, 3, PART), BF16),
            pltpu.VMEM((SEA // 8, 24, PART), F32),
            pltpu.VMEM((CHUNKS, FN, ROWS, PART), BF16),
            pltpu.VMEM(block_mask.shape, jnp.int32),
            pltpu.VMEM(state_terms.shape, F32),
            pltpu.VMEM((NBLK, M), BF16),
            dma((2 + CHUNKS,)),
            dma((count,)),
            dma((CHUNKS, SEA)),
            dma((CHUNKS, SEA)),
            dma((6 * CHUNKS,)),
            dma((6 * CHUNKS,)),
        ],
        compiler_params=pltpu.CompilerParams(collective_id=0, has_side_effects=True, vmem_limit_bytes=LIMIT_A << 20),
    )(*far_operands)
    interior, sums = pl.pallas_call(
        panel_kernel,
        out_shape=(
            jax.ShapeDtypeStruct((count, FUNCS, rows), BF16),
            pltpu.VMEM((FUNCS, LANES), F32),
        ),
        in_specs=[vmem, vmem, pl.BlockSpec(memory_space=pltpu.SMEM)],
        out_specs=(pl.BlockSpec(memory_space=pl.ANY), vmem),
        scratch_shapes=[pltpu.VMEM((UNROLL, FUNCS, rows), BF16), dma((UNROLL,))],
        compiler_params=pltpu.CompilerParams(vmem_limit_bytes=LIMIT_B << 20),
        cost_estimate=pl.CostEstimate(flops=9_700_000_000, bytes_accessed=5_000_000, transcendentals=0),
    )(rot, pext, connectivity)
    grad = pl.pallas_call(
        gradient_kernel,
        out_shape=jax.ShapeDtypeStruct((3, NV // LANES, LANES), F32),
        in_specs=[vmem, vmem],
        out_specs=vmem,
        scratch_shapes=[
            pltpu.VMEM((FN, 2 * SEA, LANES), F32),
            pltpu.VMEM((FN, 2 * SEA, LANES), F32),
            pltpu.VMEM((8 * SEA, LANES), F32),
            pltpu.VMEM((8 * SEA, LANES), F32),
            dma((FN,)),
            dma((FN,)),
            dma((SEA,)),
            dma((SEA,)),
        ],
        compiler_params=pltpu.CompilerParams(collective_id=1, has_side_effects=True, vmem_limit_bytes=8 << 20),
    )(sums, var_map.T)
    return interior, grad.reshape(3, NV)


def solution(mesh):
    placed = (
        P(("fn", "se"), None),
        P("se", "fn", None),
        P("se", "fn", None),
        P("se", None),
        P("se", "fn"),
        P("se", "fn"),
    )
    return jax.shard_map(
        body,
        mesh=mesh,
        in_specs=placed,
        out_specs=(P("se", None, "fn"), P(("fn", "se"), None)),
        check_vma=False,
    )
```
